512 devices in a mesh: fsdp: 32 (over z_hi, x, core), tp: 16 (over y, z_lo).
Axes of the slice: x: 4, y: 4, z: 16 (z_hi: 4, z_lo: 4; z = z_hi * 4 + z_lo), core: 2. Of those that a mesh axis runs over, the one named last changes fastest.
Arguments:
- tokens: bfloat16 [8192, 4096], P(('fsdp', 'tp')), may hold values from -6 to 6
- gate_weight: bfloat16 [4096, 14336], P('fsdp', 'tp'), may hold values from -0.09375 to 0.09375
- up_weight: bfloat16 [4096, 14336], P('fsdp', 'tp'), may hold values from -0.09375 to 0.09375
- canon_taps: float32 [2, 4, 14336], P(None, None, 'tp'), may hold values from -2 to 2
Outputs:
- hidden: bfloat16 [8192, 14336], P('fsdp', 'tp')
The draws below stay inside these ranges and needn't reach their ends.
All inputs are finite; a program needn't handle non-finite values.
Results may differ from the reference program's by a relative error of at most 0.002.
Values may be sent and summed in bfloat16 or wider, within the bound.
A program may use at most 64 MiB of HBM per device.

```python
import jax
import jax.numpy as jnp
from jax import lax

D = 4096
FF = 14336
TAPS = 4
TOK_DEV = 256
TOKENS = 8192
N_FSDP = 32


def block_scale(own_key, dims, cuts, smallest, largest):
    loudness = 1.0
    for dim, parts in cuts:
        draws = jax.random.uniform(jax.random.fold_in(jax.random.fold_in(own_key, 6), dim), (parts,), jnp.float32, smallest / len(cuts), largest / len(cuts))
        loudness = loudness * jnp.repeat(jnp.exp(draws), dims[dim] // parts).reshape((-1,) + (1,) * (len(dims) - 1 - dim))
    return loudness


def gaussian(stream_key, dims, spread, bound, shards=(), kind=jnp.bfloat16):
    level = block_scale(stream_key, dims, shards, -0.22, 0.18) if shards else 1.0
    drawn = jax.random.normal(stream_key, dims, jnp.float32) * spread * level
    return jnp.minimum(jnp.maximum(drawn, -bound), bound).astype(kind)


def setup_inputs(seed: int = 0) -> dict:
    keys = jax.random.split(jax.random.key(seed), 5)
    return {
        "tokens": gaussian(keys[0], (TOKENS, D), 1.0, 6.0, ((0, 512),)),
        "gate_weight": gaussian(keys[1], (D, FF), D ** -0.5, 0.09375, ((0, 32), (1, 16))),
        "up_weight": gaussian(keys[2], (D, FF), D ** -0.5, 0.09375, ((0, 32), (1, 16))),
        "canon_taps": gaussian(keys[3], (2, TAPS, FF), 0.35, 2.0, ((2, 16),), jnp.float32),
    }


def canon_mix(projected, taps):
    length = projected.shape[0]
    padded = jnp.pad(projected, ((3, 0), (0, 0)))
    mixed = projected
    for tap in range(4):
        mixed = mixed + taps[tap] * padded[3 - tap:3 - tap + length]
    return mixed


def reference(tokens, gate_weight, up_weight, canon_taps):
    grouped = tokens.reshape(N_FSDP, TOK_DEV, D)

    def per_group(group_rows):
        gate = jnp.dot(group_rows, gate_weight, preferred_element_type=jnp.float32)
        up = jnp.dot(group_rows, up_weight, preferred_element_type=jnp.float32)
        mixed_gate = canon_mix(gate, canon_taps[0])
        mixed_up = canon_mix(up, canon_taps[1])
        return (jax.nn.silu(mixed_gate) * mixed_up).astype(jnp.bfloat16)

    result = lax.map(per_group, grouped)
    return result.reshape(TOKENS, FF)
```

```python
import jax
import jax.numpy as jnp
from jax import lax
from jax.experimental import pallas as pl
from jax.experimental.pallas import tpu as pltpu
from jax.sharding import PartitionSpec as P

MESH = pl.DeviceIdType.MESH
WIDTHS = (256, 256, 256, 128)
STARTS = (0, 256, 512, 768)
PARTS = len(WIDTHS)
SENDS = 192
DEPTH = 4096
GROUP = 256
STEP = 1024


def kernel(tokens, gate_w, up_w, taps, out, *scratch):
    weights = scratch[:PARTS]
    other = scratch[PARTS : 2 * PARTS]
    outgoing = scratch[2 * PARTS : 3 * PARTS]
    incoming = scratch[3 * PARTS : 4 * PARTS]
    kept = scratch[4 * PARTS : 5 * PARTS]
    result = scratch[5 * PARTS : 6 * PARTS]
    rows, total_wide, total_thin, local_sem, send_sem, weight_sem, run_sem, ring_sem, pair_sem, swap_sem = scratch[6 * PARTS :]

    f, t = lax.axis_index("fsdp"), lax.axis_index("tp")
    core = f % 2
    x = (f // 2) % 4
    z_hi = f // 8
    z_lo = t % 4
    y = t // 4
    mate = 1 - core

    def place(dz, dx, c):
        return (((z_hi + dz + 4) % 4) * 4 + (x + dx + 4) % 4) * 2 + c

    sibling = (place(0, 0, mate), t)

    def along_z(dz, c):
        return (place(dz, 0, c), t)

    def along_x(dx, c):
        return (place(0, dx, c), t)

    def along_y(dy):
        return (f, ((y + dy + 4) % 4) * 4 + z_lo)

    def along_run(d):
        return (f, y * 4 + (z_lo + d + 4) % 4)

    own_rows = pl.ds(pl.multiple_of(core * GROUP + t * 16, 16), 16)
    row_copy = pltpu.make_async_copy(tokens, rows.at[own_rows], local_sem.at[2 * PARTS])
    staged = []
    for j in range(PARTS):
        cols = pl.ds(STARTS[j], WIDTHS[j])
        staged.append(
            (
                pltpu.make_async_copy(gate_w.at[:, cols], weights[j].at[f], local_sem.at[2 * j]),
                pltpu.make_async_copy(up_w.at[:, cols], other[j], local_sem.at[2 * j + 1]),
                pltpu.make_async_copy(up_w.at[:, cols], weights[j].at[f], local_sem.at[2 * j]),
                pltpu.make_async_copy(gate_w.at[:, cols], other[j], local_sem.at[2 * j + 1]),
            )
        )

    @pl.when(core == 0)
    def _():
        for j in range(PARTS):
            staged[j][0].start()
            staged[j][1].start()

    @pl.when(core == 1)
    def _():
        for j in range(PARTS):
            staged[j][2].start()
            staged[j][3].start()

    row_copy.start()

    barrier = pltpu.get_barrier_semaphore()
    partners = [sibling]
    for c in range(2):
        for d in (1, -1):
            partners.append(along_z(d, c))
            partners.append(along_x(d, c))
    for d in (1, -1):
        partners.append(along_y(d))
        partners.append(along_run(d))
    for device in partners:
        pl.semaphore_signal(barrier, inc=1, device_id=device, device_id_type=MESH)
    pl.semaphore_wait(barrier, len(partners))

    pending = []
    counter = [0]

    def send(src, dst, arrive, device):
        copy = pltpu.make_async_remote_copy(
            src_ref=src,
            dst_ref=dst,
            send_sem=send_sem.at[counter[0]],
            recv_sem=arrive,
            device_id=device,
            device_id_type=MESH,
        )
        counter[0] += 1
        copy.start()
        return copy

    def post(src, dst, arrive, device):
        pending.append(send(src, dst, arrive, device))

    def landed(ref, arrive):
        pltpu.make_async_remote_copy(
            src_ref=ref, dst_ref=ref, send_sem=send_sem.at[0], recv_sem=arrive, device_id=sibling, device_id_type=MESH
        ).wait_recv()

    def await_slot(j, slot):
        landed(weights[j].at[slot], weight_sem.at[slot, j])

    def forward(j, slot, device):
        post(weights[j].at[slot], weights[j].at[slot], weight_sem.at[slot, j], device)

    def send_other(j, device):
        post(other[j], weights[j].at[f], weight_sem.at[f, j], device)

    def pair_slots(kind, dx):
        if kind == "own":
            return place(0, dx, core), place(0, dx, mate)
        if kind == "near":
            return place(-1, dx, core), place(1, dx, mate)
        if kind == "rest":
            return place(-1, dx, mate), place(1, dx, core)
        return place(2, dx, core), place(2, dx, mate)

    def launch_z(kind, j):
        if j >= PARTS:
            return
        if kind == "near":
            forward(j, f, along_z(1, core))
            send_other(j, along_z(-1, mate))
        else:
            send_other(j, along_z(1, mate))
            forward(j, f, along_z(-1, core))

    def arrive_column(kind, j):
        first, second = pair_slots(kind, 0)
        if kind == "own":
            return
        await_slot(j, first)
        if kind == "near":
            forward(j, first, along_z(1, core))
        forward(j, first, along_x(1, core))
        forward(j, first, along_x(-1, core))
        await_slot(j, second)
        if kind == "near":
            forward(j, second, along_z(-1, core))
        forward(j, second, along_x(1, core))
        forward(j, second, along_x(-1, core))
        if kind in ("near", "rest"):
            launch_z(kind, j + 1)

    def arrive_x(kind, j):
        below = pair_slots(kind, -1)
        above = pair_slots(kind, 1)
        await_slot(j, below[0])
        forward(j, below[0], along_x(1, core))
        await_slot(j, above[1])
        forward(j, above[1], along_x(-1, core))
        await_slot(j, below[1])
        await_slot(j, above[0])

    def arrive_far(kind, j):
        far = pair_slots(kind, 2)
        await_slot(j, far[0])
        await_slot(j, far[1])
        if kind == "own":
            await_slot(j, sibling[0])

    def run_rows(index):
        return pl.ds(pl.multiple_of(core * GROUP + y * 64 + index * 16, 16), 16)

    def block_rows(dy, offset=0, size=64):
        return pl.ds(pl.multiple_of(core * GROUP + ((y + dy + 4) % 4) * 64 + offset, 16), size)

    def mate_rows(dy):
        return pl.ds(pl.multiple_of(mate * GROUP + ((y + dy + 4) % 4) * 64, 16), 64)

    run_sends = []

    def run_send(condition, index, d, sem_index):
        @pl.when(condition)
        def _():
            pltpu.make_async_remote_copy(
                src_ref=rows.at[run_rows(index)],
                dst_ref=rows.at[run_rows(index)],
                send_sem=run_sem.at[4 + sem_index],
                recv_sem=run_sem.at[index],
                device_id=along_run(d),
                device_id_type=MESH,
            ).start()

        run_sends.append((condition, index, d, sem_index))

    def finish_run_sends():
        for condition, index, d, sem_index in run_sends:

            @pl.when(condition)
            def _():
                pltpu.make_async_remote_copy(
                    src_ref=rows.at[run_rows(index)],
                    dst_ref=rows.at[run_rows(index)],
                    send_sem=run_sem.at[4 + sem_index],
                    recv_sem=run_sem.at[index],
                    device_id=along_run(d),
                    device_id_type=MESH,
                ).wait_send()

    def tokens_start():
        run_send(z_lo < 3, z_lo, 1, 0)
        run_send(z_lo > 0, z_lo, -1, 1)

    def tokens_run(d):
        @pl.when(z_lo >= d)
        def _():
            landed(rows.at[run_rows(z_lo - d)], run_sem.at[z_lo - d])

        if d < 3:
            run_send((z_lo >= d) & (z_lo < 3), z_lo - d, 1, 2 * d)

        @pl.when(z_lo + d <= 3)
        def _():
            landed(rows.at[run_rows(z_lo + d)], run_sem.at[z_lo + d])

        if d < 3:
            run_send((z_lo + d <= 3) & (z_lo > 0), z_lo + d, -1, 2 * d + 1)

    def to_mate(dy, index):
        post(rows.at[block_rows(dy)], rows.at[block_rows(dy)], pair_sem.at[index], sibling)

    def tokens_ring_start():
        block = rows.at[block_rows(0)]
        post(block, block, ring_sem.at[0], along_y(1))
        post(block, block, ring_sem.at[1], along_y(-1))
        to_mate(0, 0)

    def tokens_ring_relay():
        landed(rows.at[block_rows(-1)], ring_sem.at[0])
        half = rows.at[block_rows(-1, 0, 32)]
        post(half, half, ring_sem.at[2], along_y(1))
        landed(rows.at[block_rows(1)], ring_sem.at[1])
        half = rows.at[block_rows(1, 32, 32)]
        post(half, half, ring_sem.at[3], along_y(-1))
        to_mate(-1, 1)
        to_mate(1, 2)

    def tokens_ring_end():
        landed(rows.at[block_rows(2, 0, 32)], ring_sem.at[2])
        landed(rows.at[block_rows(2, 32, 32)], ring_sem.at[3])
        to_mate(2, 3)

    def tokens_mate():
        for index, dy in enumerate((0, -1, 1, 2)):
            landed(rows.at[mate_rows(dy)], pair_sem.at[index])

    swaps = []

    def compute(j):
        width = WIDTHS[j]
        total = total_wide if width == 256 else total_thin
        for g in range(2):
            total[g, 0:8, :] = jnp.zeros((8, width), jnp.float32)
            total[g, 8 : 8 + GROUP, :] = jnp.zeros((GROUP, width), jnp.float32)

        def multiply(i, carry):
            at = pl.multiple_of(i * STEP, STEP)
            block = weights[j][pl.ds(i * (STEP // 128), STEP // 128)].reshape(STEP, width)
            product = jnp.dot(rows[:, pl.ds(at, STEP)], block, preferred_element_type=jnp.float32)
            total[0, 8 : 8 + GROUP, :] += product[:GROUP]
            total[1, 8 : 8 + GROUP, :] += product[GROUP:]
            return carry

        lax.fori_loop(0, DEPTH // STEP, multiply, 0)
        tap = [taps[core, k : k + 1, STARTS[j] : STARTS[j] + width] for k in range(4)]

        def mix(group, target):
            for r in range(0, GROUP, 32):
                mixed = total[group, 8 + r : 40 + r, :]
                mixed = mixed + tap[0] * mixed
                for k in range(1, 4):
                    mixed = mixed + tap[k] * total[group, 8 + r - k : 40 + r - k, :]
                active = mixed / (1.0 + jnp.exp(-mixed))
                target[r : r + 32, :] = jnp.where(core == 0, active, mixed)

        mix(mate, outgoing[j])
        swaps.append(send(outgoing[j], incoming[j], swap_sem.at[j], sibling))
        mix(core, kept[j])

    def store(j):
        return pltpu.make_async_copy(result[j], out.at[:, pl.ds(STARTS[j], WIDTHS[j])], local_sem.at[2 * PARTS + 1 + j])

    def finish(j):
        landed(incoming[j], swap_sem.at[j])
        result[j][...] = (kept[j][...] * incoming[j][...]).astype(jnp.bfloat16)
        store(j).start()

    for j in range(PARTS):
        staged[j][0].wait()
        staged[j][1].wait()
        if j == 0:
            launch_z("near", 0)
            launch_z("rest", 0)
            row_copy.wait()
            tokens_start()
        forward(j, f, along_x(1, core))
        forward(j, f, along_x(-1, core))
        send_other(j, along_x(1, mate))
        send_other(j, along_x(-1, mate))
        send_other(j, sibling)

    order = [("own", 0), ("own", 1), ("near", 0), ("own", 2), ("rest", 0), ("own", 3), ("far", 0)]
    for j in range(1, PARTS):
        order += [("near", j), ("rest", j), ("far", j)]
    extra = {
        0: [lambda: tokens_run(1)],
        1: [lambda: tokens_run(2)],
        2: [lambda: tokens_run(3), tokens_ring_start],
        5: [tokens_ring_relay],
        7: [tokens_ring_end],
        9: [tokens_mate, lambda: compute(0)],
        11: [lambda: finish(0)],
        12: [lambda: compute(1)],
        14: [lambda: finish(1)],
        15: [lambda: compute(2)],
        17: [lambda: finish(2), lambda: compute(3), lambda: finish(3)],
    }
    last = len(order)
    waited = 0
    marks = []
    for s in range(last + 2):
        if s < last:
            arrive_column(*order[s])
        if 1 <= s <= last:
            arrive_x(*order[s - 1])
        if s >= 2:
            arrive_far(*order[s - 2])
        if s == last + 1:
            for copy in pending[waited:]:
                copy.wait_send()
            finish_run_sends()
        elif s >= 6:
            limit = marks[s - 6]
            for copy in pending[waited:limit]:
                copy.wait_send()
            waited = max(waited, limit)
        marks.append(len(pending))
        for action in extra.get(s, []):
            action()
    for copy in swaps:
        copy.wait_send()
    for j in range(PARTS):
        store(j).wait()


def on_device(tokens, gate_weight, up_weight, canon_taps):
    anywhere = pl.BlockSpec(memory_space=pl.ANY)
    slots = 32
    scratch = [pltpu.VMEM((slots, 128, w), jnp.bfloat16) for w in WIDTHS]
    scratch += [pltpu.VMEM((128, w), jnp.bfloat16) for w in WIDTHS]
    for _ in range(3):
        scratch += [pltpu.VMEM((GROUP, w), jnp.float32) for w in WIDTHS]
    scratch += [pltpu.VMEM((GROUP, w), jnp.bfloat16) for w in WIDTHS]
    scratch += [
        pltpu.VMEM((2 * GROUP, DEPTH), jnp.bfloat16),
        pltpu.VMEM((2, GROUP + 8, 256), jnp.float32),
        pltpu.VMEM((2, GROUP + 8, 128), jnp.float32),
        pltpu.SemaphoreType.DMA((3 * PARTS + 1,)),
        pltpu.SemaphoreType.DMA((SENDS,)),
        pltpu.SemaphoreType.DMA((slots, PARTS)),
        pltpu.SemaphoreType.DMA((10,)),
        pltpu.SemaphoreType.DMA((4,)),
        pltpu.SemaphoreType.DMA((4,)),
        pltpu.SemaphoreType.DMA((PARTS,)),
    ]
    return pl.pallas_call(
        kernel,
        out_shape=jax.ShapeDtypeStruct((GROUP, gate_weight.shape[1]), jnp.bfloat16),
        in_specs=[anywhere, anywhere, anywhere, pl.BlockSpec(memory_space=pltpu.VMEM)],
        out_specs=anywhere,
        scratch_shapes=scratch,
        compiler_params=pltpu.CompilerParams(collective_id=0, has_side_effects=True, vmem_limit_bytes=48 * 1024 * 1024),
        cost_estimate=pl.CostEstimate(flops=2 * 512 * 4096 * 896, bytes_accessed=1 << 20, transcendentals=512 * 896),
    )(tokens, gate_weight, up_weight, canon_taps)


def solution(mesh):
    in_specs = (P(("fsdp", "tp"), None), P("fsdp", "tp"), P("fsdp", "tp"), P(None, None, "tp"))
    return jax.shard_map(on_device, mesh=mesh, in_specs=in_specs, out_specs=P("fsdp", "tp"), check_vma=False)
```

```python
import jax
import jax.numpy as jnp
from jax import lax
from jax.experimental import pallas as pl
from jax.experimental.pallas import tpu as pltpu
from jax.sharding import PartitionSpec as P

MESH = pl.DeviceIdType.MESH
WIDTHS = (256, 128, 128)
OFFSETS = (0, 256, 384)
PARTS = len(WIDTHS)
SENDS = 160
DEPTH = 4096
GROUP = 256
STEP = 2048
WINDOW = 3


def kernel(tokens, gate_w, up_w, taps, out, *scratch):
    weights = scratch[:PARTS]
    other = scratch[PARTS : 2 * PARTS]
    away = scratch[2 * PARTS : 3 * PARTS]
    other_away = scratch[3 * PARTS : 4 * PARTS]
    outgoing = scratch[4 * PARTS : 5 * PARTS]
    incoming = scratch[5 * PARTS : 6 * PARTS]
    kept = scratch[6 * PARTS : 7 * PARTS]
    result = scratch[7 * PARTS : 8 * PARTS]
    rows, total_wide, total_thin, local_sem, send_sem, weight_sem, run_sem, run_send_sem, ring_sem, ring_send_sem, far_sem, pair_sem, swap_sem, back_sem = scratch[
        8 * PARTS :
    ]

    f, t = lax.axis_index("fsdp"), lax.axis_index("tp")
    core = f % 2
    mate = 1 - core
    x = (f // 2) % 4
    z_hi = f // 8
    z_lo = t % 4
    y = t // 4
    half = (z_hi // 2 + z_lo) % 2
    other_half = 1 - half
    upper = 1 - z_hi % 2
    position = upper * 4 + z_lo
    z_same = (z_hi + 2 * upper - 1 + 4) % 4
    z_rows = (z_hi - 2 * upper + 1 + 4) % 4
    z_across = (z_hi + 2) % 4
    z = z_hi * 4 + z_lo

    def slot(zz, dx, c):
        return (zz * 4 + (x + dx + 4) % 4) * 2 + c

    def at_z(zz, c):
        return (slot(zz, 0, c), t)

    def along_x(d, c):
        return (slot(z_hi, d, c), t)

    def along_y(d):
        return (f, ((y + d + 4) % 4) * 4 + z_lo)

    def along_line(d):
        there = (z + d + 16) % 16
        return (slot(there // 4, 0, core), y * 4 + there % 4)

    sibling = at_z(z_hi, mate)

    def present(j, of_half, body):
        if j < 2:
            body()
        else:
            pl.when(of_half == 0)(body)

    def begin(of_half, j):
        return pl.ds(pl.multiple_of(of_half * 512 + OFFSETS[j], 128), WIDTHS[j])

    def row_at(q):
        return pl.ds(pl.multiple_of((q // 4) * 512 + core * GROUP + y * 64 + (q % 4) * 16, 16), 16)

    row_copy = pltpu.make_async_copy(tokens, rows.at[row_at(position)], local_sem.at[4 * PARTS])
    row_copy.start()

    def stage(j, mine, theirs):
        def near():
            pltpu.make_async_copy(mine.at[:, begin(half, j)], weights[j].at[f], local_sem.at[4 * j]).start()
            pltpu.make_async_copy(theirs.at[:, begin(half, j)], other[j], local_sem.at[4 * j + 1]).start()

        def far():
            pltpu.make_async_copy(mine.at[:, begin(1 - half, j)], away[j], local_sem.at[4 * j + 2]).start()
            pltpu.make_async_copy(theirs.at[:, begin(1 - half, j)], other_away[j], local_sem.at[4 * j + 3]).start()

        present(j, half, near)
        present(j, 1 - half, far)

    @pl.when(core == 0)
    def _():
        for j in range(PARTS):
            stage(j, gate_w, up_w)

    @pl.when(core == 1)
    def _():
        for j in range(PARTS):
            stage(j, up_w, gate_w)

    def staged(j):
        def near():
            pltpu.make_async_copy(gate_w.at[:, begin(half, j)], weights[j].at[f], local_sem.at[4 * j]).wait()
            pltpu.make_async_copy(gate_w.at[:, begin(half, j)], other[j], local_sem.at[4 * j + 1]).wait()

        def far():
            pltpu.make_async_copy(gate_w.at[:, begin(1 - half, j)], away[j], local_sem.at[4 * j + 2]).wait()
            pltpu.make_async_copy(gate_w.at[:, begin(1 - half, j)], other_away[j], local_sem.at[4 * j + 3]).wait()

        present(j, half, near)
        present(j, 1 - half, far)

    barrier = pltpu.get_barrier_semaphore()
    partners = [sibling]
    for c in (core, mate):
        partners += [at_z(z_same, c), at_z(z_rows, c), along_x(1, c), along_x(-1, c)]
    partners += [along_line(1), along_line(-1), along_y(1), along_y(-1)]
    for device in partners:
        pl.semaphore_signal(barrier, inc=1, device_id=device, device_id_type=MESH)
    pl.semaphore_wait(barrier, len(partners))

    counter = [0]
    pending = []

    def remote(src, dst, leave, arrive, device):
        return pltpu.make_async_remote_copy(
            src_ref=src, dst_ref=dst, send_sem=leave, recv_sem=arrive, device_id=device, device_id_type=MESH
        )

    def post(src, dst, arrive, device, like, guard=None):
        copy = remote(src, dst, send_sem.at[counter[0]], arrive, device)
        pending.append((guard, counter[0], like))
        counter[0] += 1
        copy.start()

    def landed(ref, arrive):
        remote(ref, ref, send_sem.at[0], arrive, sibling).wait_recv()

    def settle():
        for guard, index, like in pending:
            copy = remote(like(), like(), send_sem.at[index], send_sem.at[index], sibling)
            if guard is None:
                copy.wait_send()
            else:
                pl.when(guard == 0)(copy.wait_send)
        pending.clear()

    def guard_of(j, of_half):
        return None if j < 2 else of_half

    def send_own(j):
        def near():
            guard = guard_of(j, half)
            mine, arrive = weights[j].at[f], weight_sem.at[f, j]
            post(mine, mine, arrive, at_z(z_same, core), lambda: weights[j].at[0], guard)
            post(other[j], mine, arrive, at_z(z_same, mate), lambda: weights[j].at[0], guard)

        def far():
            guard = guard_of(j, other_half)
            post(away[j], weights[j].at[f], weight_sem.at[f, j], at_z(z_rows, core), lambda: weights[j].at[0], guard)
            post(other_away[j], weights[j].at[f], weight_sem.at[f, j], at_z(z_rows, mate), lambda: weights[j].at[0], guard)

        present(j, half, near)
        present(j, 1 - half, far)

    def spread_own(j):
        def body():
            guard = guard_of(j, half)
            mine, arrive = weights[j].at[f], weight_sem.at[f, j]
            for d in (1, -1):
                post(mine, mine, arrive, along_x(d, core), lambda: weights[j].at[0], guard)
                post(other[j], mine, arrive, along_x(d, mate), lambda: weights[j].at[0], guard)
            post(other[j], mine, arrive, sibling, lambda: weights[j].at[0], guard)

        present(j, half, body)

    def pair(j, zz, dx):
        at = slot(zz, dx, 0)
        return weights[j].at[pl.ds(at, 2)], weight_sem.at[at, j]

    def both(j, zz, dx):
        for c in (core, mate):
            landed(weights[j].at[slot(zz, dx, c)], weight_sem.at[slot(zz, dx, c), j])

    def spread(j, zz):
        ref, arrive = pair(j, zz, 0)
        for d in (1, -1):
            post(ref, ref, arrive, along_x(d, core), lambda: weights[j].at[pl.ds(0, 2)], guard_of(j, half))

    def from_rows(j):
        def body():
            both(j, z_rows, 0)
            ref, arrive = pair(j, z_rows, 0)
            post(ref, ref, arrive, at_z(z_same, core), lambda: weights[j].at[pl.ds(0, 2)], guard_of(j, half))
            spread(j, z_rows)

        present(j, half, body)

    def from_same(j):
        def body():
            both(j, z_same, 0)
            spread(j, z_same)

        present(j, half, body)

    def from_across(j):
        def body():
            landed(*pair(j, z_across, 0))
            spread(j, z_across)

        present(j, half, body)

    def side(j, zz):
        def body():
            for d, c in ((1, core), (-1, mate)):
                if zz is z_hi:
                    both(j, z_hi, -d)
                else:
                    landed(*pair(j, zz, -d))
                at = slot(zz, -d, c)
                ref = weights[j].at[at]
                post(ref, ref, weight_sem.at[at, j], along_x(d, core), lambda: weights[j].at[0], guard_of(j, half))

        present(j, half, body)

    def gathered(j):
        landed(weights[j].at[slot(z_hi, 0, mate)], weight_sem.at[slot(z_hi, 0, mate), j])
        for zz in (z_hi, z_rows, z_same, z_across):
            both(j, zz, 2)

    ring = (1, -1)
    line_sends = []

    def line_copy(q, d, index):
        ref = rows.at[row_at(q)]
        return remote(ref, ref, run_send_sem.at[index], run_sem.at[q], along_line(d))

    def ring_copy(q, way):
        ref = rows.at[row_at(q)]
        return remote(ref, ref, ring_send_sem.at[q, way], ring_sem.at[q, way], along_y(ring[way]))

    def line_send(condition, q, d, index):
        pl.when(condition)(lambda: line_copy(q, d, index).start())
        line_sends.append((condition, q, d, index))

    def take(condition, q):
        @pl.when(condition)
        def _():
            landed(rows.at[row_at(q)], run_sem.at[q])

    def give(condition, q):
        @pl.when(condition)
        def _():
            for way in range(2):
                ring_copy(q, way).start()

    def line_start():
        line_send(position < 7, position, 1, 0)
        line_send(position > 0, position, -1, 1)
        for way in range(2):
            ring_copy(position, way).start()

    def line_step(d):
        take(position >= d, position - d)
        if d < 7:
            line_send((position >= d) & (position < 7), position - d, 1, 2 * d)
        take(position + d <= 7, position + d)
        if d < 7:
            line_send((position + d <= 7) & (position > 0), position + d, -1, 2 * d + 1)
        give(position >= d, position - d)
        give(position + d <= 7, position + d)

    def line_settle():
        for condition, q, d, index in line_sends:
            pl.when(condition)(line_copy(q, d, index).wait_send)

        def wait_ring(q, carry):
            for way in range(2):
                ring_copy(q, way).wait_send()
            return carry

        lax.fori_loop(0, 8, wait_ring, 0)

    def block(u, c, dy):
        return rows.at[pl.ds(pl.multiple_of(u * 512 + c * GROUP + ((y + dy + 4) % 4) * 64, 64), 64)]

    def to_mate(u, index, dy):
        post(block(u, core, dy), block(u, core, dy), pair_sem.at[u, index], sibling, lambda: rows.at[pl.ds(0, 64)])

    def far_half(u, dy, way):
        at = u * 512 + core * GROUP + ((y + dy + 4) % 4) * 64 + 32 * way
        return rows.at[pl.ds(pl.multiple_of(at, 32), 32)]

    def ring_relay(u):
        for way, d in enumerate(ring):
            for i in range(4):
                at = u * 512 + core * GROUP + ((y - d + 4) % 4) * 64 + i * 16
                landed(rows.at[pl.ds(pl.multiple_of(at, 16), 16)], ring_sem.at[u * 4 + i, way])
            ref = far_half(u, -d, way)
            post(ref, ref, far_sem.at[u, way], along_y(d), lambda: rows.at[pl.ds(0, 32)])
        to_mate(u, 3, 0)
        for way, d in enumerate(ring):
            to_mate(u, way, -d)

    def ring_end(u):
        for way in range(2):
            landed(far_half(u, 2, way), far_sem.at[u, way])
        to_mate(u, 2, 2)

    def tokens_end():
        for u in range(2):
            for index, dy in enumerate((-1, 1, 2, 0)):
                landed(block(u, mate, dy), pair_sem.at[u, index])

    def compute(j):
        width = WIDTHS[j]
        total = total_wide if width == 256 else total_thin

        def body():
            gathered(j)
            for g in range(4):
                total[g, 0:8, :] = jnp.zeros((8, width), jnp.float32)
            for i in range(0, DEPTH, STEP):
                part = weights[j][i // 128 : (i + STEP) // 128].reshape(STEP, width)
                product = jnp.dot(rows[:, i : i + STEP], part, preferred_element_type=jnp.float32)
                for g in range(4):
                    if i == 0:
                        total[g, 8 : 8 + GROUP, :] = product[g * GROUP : (g + 1) * GROUP]
                    else:
                        total[g, 8 : 8 + GROUP, :] += product[g * GROUP : (g + 1) * GROUP]
            tap = [taps[core, k : k + 1, begin(half, j)] for k in range(4)]

            def mix(c, target):
                for u in range(2):
                    group = u * 2 + c
                    for r in range(0, GROUP, 32):
                        mixed = total[group, 8 + r : 40 + r, :]
                        mixed = mixed + tap[0] * mixed
                        for k in range(1, 4):
                            mixed = mixed + tap[k] * total[group, 8 + r - k : 40 + r - k, :]
                        active = mixed / (1.0 + jnp.exp(-mixed))
                        target[u, r : r + 32, :] = jnp.where(core == 0, active, mixed)

            mix(mate, outgoing[j])
            post(outgoing[j], incoming[j], swap_sem.at[j], sibling, lambda: outgoing[j], guard_of(j, half))
            mix(core, kept[j])

        present(j, half, body)

    def store(j):
        return pltpu.make_async_copy(result[j].at[upper], out.at[:, begin(half, j)], local_sem.at[4 * PARTS + 1 + j])

    def finish(j):
        def body():
            landed(incoming[j], swap_sem.at[j])
            result[j][...] = (kept[j][...] * incoming[j][...]).astype(jnp.bfloat16)
            post(result[j].at[1 - upper], out.at[:, begin(half, j)], back_sem.at[j], at_z(z_rows, core), lambda: result[j].at[0], guard_of(j, half))
            store(j).start()

        present(j, half, body)

    row_copy.wait()
    line_start()
    staged(0)
    send_own(0)
    spread_own(0)
    for j in range(1, PARTS):
        staged(j)
        if j < WINDOW:
            send_own(j)
        spread_own(j)
    line_step(1)
    line_step(2)
    side(0, z_hi)
    from_rows(0)
    if WINDOW < 2:
        send_own(1)
    line_step(3)
    from_same(0)
    if WINDOW < 3:
        send_own(2)
    side(0, z_rows)
    line_step(4)
    side(1, z_hi)
    side(0, z_same)
    line_step(5)
    side(2, z_hi)
    from_across(0)
    ring_relay(upper)
    line_step(6)
    from_rows(1)
    line_step(7)
    side(0, z_across)
    from_same(1)
    side(1, z_rows)
    from_rows(2)
    ring_end(upper)
    ring_relay(1 - upper)
    side(1, z_same)
    from_same(2)
    from_across(1)
    side(2, z_rows)
    side(2, z_same)
    side(1, z_across)
    ring_end(1 - upper)
    tokens_end()
    compute(0)
    from_across(2)
    finish(0)
    side(2, z_across)
    compute(1)
    finish(1)
    compute(2)
    finish(2)
    settle()
    line_settle()
    for j in range(PARTS):
        present(j, half, lambda j=j: store(j).wait())
    for j in range(PARTS):
        present(j, 1 - half, lambda j=j: landed(out.at[:, begin(1 - half, j)], back_sem.at[j]))


def on_device(tokens, gate_weight, up_weight, canon_taps):
    anywhere = pl.BlockSpec(memory_space=pl.ANY)
    slots = 32
    scratch = [pltpu.VMEM((slots, 128, w), jnp.bfloat16) for w in WIDTHS]
    for _ in range(3):
        scratch += [pltpu.VMEM((128, w), jnp.bfloat16) for w in WIDTHS]
    for _ in range(3):
        scratch += [pltpu.VMEM((2, GROUP, w), jnp.float32) for w in WIDTHS]
    scratch += [pltpu.VMEM((2, GROUP, w), jnp.bfloat16) for w in WIDTHS]
    scratch += [
        pltpu.VMEM((4 * GROUP, DEPTH), jnp.bfloat16),
        pltpu.VMEM((4, GROUP + 8, 256), jnp.float32),
        pltpu.VMEM((4, GROUP + 8, 128), jnp.float32),
        pltpu.SemaphoreType.DMA((5 * PARTS + 1,)),
        pltpu.SemaphoreType.DMA((SENDS,)),
        pltpu.SemaphoreType.DMA((slots, PARTS)),
        pltpu.SemaphoreType.DMA((8,)),
        pltpu.SemaphoreType.DMA((14,)),
        pltpu.SemaphoreType.DMA((8, 2)),
        pltpu.SemaphoreType.DMA((8, 2)),
        pltpu.SemaphoreType.DMA((2, 2)),
        pltpu.SemaphoreType.DMA((2, 4)),
        pltpu.SemaphoreType.DMA((PARTS,)),
        pltpu.SemaphoreType.DMA((PARTS,)),
    ]
    return pl.pallas_call(
        kernel,
        out_shape=jax.ShapeDtypeStruct((GROUP, gate_weight.shape[1]), jnp.bfloat16),
        in_specs=[anywhere, anywhere, anywhere, pl.BlockSpec(memory_space=pltpu.VMEM)],
        out_specs=anywhere,
        scratch_shapes=scratch,
        compiler_params=pltpu.CompilerParams(collective_id=0, has_side_effects=True, vmem_limit_bytes=56 * 1024 * 1024),
        cost_estimate=pl.CostEstimate(flops=2 * 1024 * 4096 * 512, bytes_accessed=1 << 20, transcendentals=512 * 896),
    )(tokens, gate_weight, up_weight, canon_taps)


def solution(mesh):
    in_specs = (P(("fsdp", "tp"), None), P("fsdp", "tp"), P("fsdp", "tp"), P(None, None, "tp"))
    return jax.shard_map(on_device, mesh=mesh, in_specs=in_specs, out_specs=P("fsdp", "tp"), check_vma=False)
```

```python
import jax
import jax.numpy as jnp
from jax import lax
from jax.experimental import pallas as pl
from jax.experimental.pallas import tpu as pltpu
from jax.sharding import PartitionSpec as P

MESH = pl.DeviceIdType.MESH
WIDTHS = (256, 128, 128)
OFFSETS = (0, 256, 384)
PARTS = len(WIDTHS)
SENDS = 160
DEPTH = 4096
GROUP = 256
STEP = 2048
WINDOW = 3


def kernel(tokens, gate_w, up_w, taps, out, *scratch):
    weights = scratch[:PARTS]
    other = scratch[PARTS : 2 * PARTS]
    away = scratch[2 * PARTS : 3 * PARTS]
    other_away = scratch[3 * PARTS : 4 * PARTS]
    outgoing = scratch[4 * PARTS : 5 * PARTS]
    incoming = scratch[5 * PARTS : 6 * PARTS]
    kept = scratch[6 * PARTS : 7 * PARTS]
    result = scratch[7 * PARTS : 8 * PARTS]
    rows, total_wide, total_thin, local_sem, send_sem, weight_sem, run_sem, run_send_sem, ring_sem, ring_send_sem, far_sem, pair_sem, swap_sem, back_sem = scratch[
        8 * PARTS :
    ]

    f, t = lax.axis_index("fsdp"), lax.axis_index("tp")
    core = f % 2
    mate = 1 - core
    x = (f // 2) % 4
    z_hi = f // 8
    z_lo = t % 4
    y = t // 4
    half = (z_hi // 2 + z_lo) % 2
    other_half = 1 - half
    upper = 1 - z_hi % 2
    position = upper * 4 + z_lo
    z_same = (z_hi + 2 * upper - 1 + 4) % 4
    z_rows = (z_hi - 2 * upper + 1 + 4) % 4
    z_across = (z_hi + 2) % 4
    z = z_hi * 4 + z_lo

    def slot(zz, dx, c):
        return (zz * 4 + (x + dx + 4) % 4) * 2 + c

    def at_z(zz, c):
        return (slot(zz, 0, c), t)

    def along_x(d, c):
        return (slot(z_hi, d, c), t)

    def along_y(d):
        return (f, ((y + d + 4) % 4) * 4 + z_lo)

    def along_line(d):
        there = (z + d + 16) % 16
        return (slot(there // 4, 0, core), y * 4 + there % 4)

    sibling = at_z(z_hi, mate)

    def present(j, of_half, body):
        if j < 2:
            body()
        else:
            pl.when(of_half == 0)(body)

    def begin(of_half, j):
        return pl.ds(pl.multiple_of(of_half * 512 + OFFSETS[j], 128), WIDTHS[j])

    def row_at(q):
        return pl.ds(pl.multiple_of((q // 4) * 512 + core * GROUP + y * 64 + (q % 4) * 16, 16), 16)

    row_copy = pltpu.make_async_copy(tokens, rows.at[row_at(position)], local_sem.at[4 * PARTS])
    row_copy.start()

    def stage(j, mine, theirs):
        def near():
            pltpu.make_async_copy(mine.at[:, begin(half, j)], weights[j].at[f], local_sem.at[4 * j]).start()
            pltpu.make_async_copy(theirs.at[:, begin(half, j)], other[j], local_sem.at[4 * j + 1]).start()

        def far():
            pltpu.make_async_copy(mine.at[:, begin(1 - half, j)], away[j], local_sem.at[4 * j + 2]).start()
            pltpu.make_async_copy(theirs.at[:, begin(1 - half, j)], other_away[j], local_sem.at[4 * j + 3]).start()

        present(j, half, near)
        present(j, 1 - half, far)

    @pl.when(core == 0)
    def _():
        for j in range(PARTS):
            stage(j, gate_w, up_w)

    @pl.when(core == 1)
    def _():
        for j in range(PARTS):
            stage(j, up_w, gate_w)

    def staged(j):
        def near():
            pltpu.make_async_copy(gate_w.at[:, begin(half, j)], weights[j].at[f], local_sem.at[4 * j]).wait()
            pltpu.make_async_copy(gate_w.at[:, begin(half, j)], other[j], local_sem.at[4 * j + 1]).wait()

        def far():
            pltpu.make_async_copy(gate_w.at[:, begin(1 - half, j)], away[j], local_sem.at[4 * j + 2]).wait()
            pltpu.make_async_copy(gate_w.at[:, begin(1 - half, j)], other_away[j], local_sem.at[4 * j + 3]).wait()

        present(j, half, near)
        present(j, 1 - half, far)

    barrier = pltpu.get_barrier_semaphore()
    partners = [sibling]
    for c in (core, mate):
        partners += [at_z(z_same, c), at_z(z_rows, c), along_x(1, c), along_x(-1, c)]
    partners += [along_line(1), along_line(-1), along_y(1), along_y(-1)]
    for device in partners:
        pl.semaphore_signal(barrier, inc=1, device_id=device, device_id_type=MESH)
    pl.semaphore_wait(barrier, len(partners))

    counter = [0]
    pending = []

    def remote(src, dst, leave, arrive, device):
        return pltpu.make_async_remote_copy(
            src_ref=src, dst_ref=dst, send_sem=leave, recv_sem=arrive, device_id=device, device_id_type=MESH
        )

    def post(src, dst, arrive, device, like, guard=None):
        copy = remote(src, dst, send_sem.at[counter[0]], arrive, device)
        pending.append((guard, counter[0], like))
        counter[0] += 1
        copy.start()

    def landed(ref, arrive):
        remote(ref, ref, send_sem.at[0], arrive, sibling).wait_recv()

    def settle():
        for guard, index, like in pending:
            copy = remote(like(), like(), send_sem.at[index], send_sem.at[index], sibling)
            if guard is None:
                copy.wait_send()
            else:
                pl.when(guard == 0)(copy.wait_send)
        pending.clear()

    def guard_of(j, of_half):
        return None if j < 2 else of_half

    def send_own(j):
        def near():
            guard = guard_of(j, half)
            mine, arrive = weights[j].at[f], weight_sem.at[f, j]
            post(mine, mine, arrive, at_z(z_same, core), lambda: weights[j].at[0], guard)
            post(other[j], mine, arrive, at_z(z_same, mate), lambda: weights[j].at[0], guard)

        def far():
            guard = guard_of(j, other_half)
            post(away[j], weights[j].at[f], weight_sem.at[f, j], at_z(z_rows, core), lambda: weights[j].at[0], guard)
            post(other_away[j], weights[j].at[f], weight_sem.at[f, j], at_z(z_rows, mate), lambda: weights[j].at[0], guard)

        present(j, half, near)
        present(j, 1 - half, far)

    def spread_own(j):
        def body():
            guard = guard_of(j, half)
            mine, arrive = weights[j].at[f], weight_sem.at[f, j]
            for d in (1, -1):
                post(mine, mine, arrive, along_x(d, core), lambda: weights[j].at[0], guard)
                post(other[j], mine, arrive, along_x(d, mate), lambda: weights[j].at[0], guard)
            post(other[j], mine, arrive, sibling, lambda: weights[j].at[0], guard)

        present(j, half, body)

    def pair(j, zz, dx):
        at = slot(zz, dx, 0)
        return weights[j].at[pl.ds(at, 2)], weight_sem.at[at, j]

    def both(j, zz, dx):
        for c in (core, mate):
            landed(weights[j].at[slot(zz, dx, c)], weight_sem.at[slot(zz, dx, c), j])

    def spread(j, zz):
        ref, arrive = pair(j, zz, 0)
        for d in (1, -1):
            post(ref, ref, arrive, along_x(d, core), lambda: weights[j].at[pl.ds(0, 2)], guard_of(j, half))

    def from_rows(j):
        def body():
            both(j, z_rows, 0)
            ref, arrive = pair(j, z_rows, 0)
            post(ref, ref, arrive, at_z(z_same, core), lambda: weights[j].at[pl.ds(0, 2)], guard_of(j, half))
            spread(j, z_rows)

        present(j, half, body)

    def from_same(j):
        def body():
            both(j, z_same, 0)
            spread(j, z_same)

        present(j, half, body)

    def from_across(j):
        def body():
            landed(*pair(j, z_across, 0))
            spread(j, z_across)

        present(j, half, body)

    def side(j, zz):
        def body():
            for d, c in ((1, core), (-1, mate)):
                if zz is z_hi:
                    both(j, z_hi, -d)
                else:
                    landed(*pair(j, zz, -d))
                at = slot(zz, -d, c)
                ref = weights[j].at[at]
                post(ref, ref, weight_sem.at[at, j], along_x(d, core), lambda: weights[j].at[0], guard_of(j, half))

        present(j, half, body)

    def gathered(j):
        landed(weights[j].at[slot(z_hi, 0, mate)], weight_sem.at[slot(z_hi, 0, mate), j])
        for zz in (z_hi, z_rows, z_same, z_across):
            both(j, zz, 2)

    ring = (1, -1)
    line_sends = []

    def line_copy(q, d, index):
        ref = rows.at[row_at(q)]
        return remote(ref, ref, run_send_sem.at[index], run_sem.at[q], along_line(d))

    def ring_copy(q, way):
        ref = rows.at[row_at(q)]
        return remote(ref, ref, ring_send_sem.at[q, way], ring_sem.at[q, way], along_y(ring[way]))

    def line_send(condition, q, d, index):
        pl.when(condition)(lambda: line_copy(q, d, index).start())
        line_sends.append((condition, q, d, index))

    def take(condition, q):
        @pl.when(condition)
        def _():
            landed(rows.at[row_at(q)], run_sem.at[q])

    def give(condition, q):
        @pl.when(condition)
        def _():
            for way in range(2):
                ring_copy(q, way).start()

    def line_start():
        line_send(position < 7, position, 1, 0)
        line_send(position > 0, position, -1, 1)
        for way in range(2):
            ring_copy(position, way).start()

    def line_step(d):
        take(position >= d, position - d)
        if d < 7:
            line_send((position >= d) & (position < 7), position - d, 1, 2 * d)
        take(position + d <= 7, position + d)
        if d < 7:
            line_send((position + d <= 7) & (position > 0), position + d, -1, 2 * d + 1)
        give(position >= d, position - d)
        give(position + d <= 7, position + d)

    def line_settle():
        for condition, q, d, index in line_sends:
            pl.when(condition)(line_copy(q, d, index).wait_send)

        def wait_ring(q, carry):
            for way in range(2):
                ring_copy(q, way).wait_send()
            return carry

        lax.fori_loop(0, 8, wait_ring, 0)

    def block(u, c, dy):
        return rows.at[pl.ds(pl.multiple_of(u * 512 + c * GROUP + ((y + dy + 4) % 4) * 64, 64), 64)]

    def to_mate(u, index, dy):
        post(block(u, core, dy), block(u, core, dy), pair_sem.at[u, index], sibling, lambda: rows.at[pl.ds(0, 64)])

    def far_half(u, dy, way):
        at = u * 512 + core * GROUP + ((y + dy + 4) % 4) * 64 + 32 * way
        return rows.at[pl.ds(pl.multiple_of(at, 32), 32)]

    def ring_relay(u):
        for way, d in enumerate(ring):
            for i in range(4):
                at = u * 512 + core * GROUP + ((y - d + 4) % 4) * 64 + i * 16
                landed(rows.at[pl.ds(pl.multiple_of(at, 16), 16)], ring_sem.at[u * 4 + i, way])
            ref = far_half(u, -d, way)
            post(ref, ref, far_sem.at[u, way], along_y(d), lambda: rows.at[pl.ds(0, 32)])
        to_mate(u, 3, 0)
        for way, d in enumerate(ring):
            to_mate(u, way, -d)

    def ring_end(u):
        for way in range(2):
            landed(far_half(u, 2, way), far_sem.at[u, way])
        to_mate(u, 2, 2)

    def tokens_end():
        for u in range(2):
            for index, dy in enumerate((-1, 1, 2, 0)):
                landed(block(u, mate, dy), pair_sem.at[u, index])

    def compute(parts, guard):
        width = sum(WIDTHS[j] for j in parts)
        total = total_wide if width == 256 else total_thin
        for j in parts:
            gathered(j)
        for g in range(4):
            total[g, 0:8, :] = jnp.zeros((8, width), jnp.float32)
        for i in range(0, DEPTH, STEP):
            pieces = [weights[j][i // 128 : (i + STEP) // 128].reshape(STEP, WIDTHS[j]) for j in parts]
            part = pieces[0] if len(pieces) == 1 else jnp.concatenate(pieces, axis=1)
            product = jnp.dot(rows[:, i : i + STEP], part, preferred_element_type=jnp.float32)
            for g in range(4):
                if i == 0:
                    total[g, 8 : 8 + GROUP, :] = product[g * GROUP : (g + 1) * GROUP]
                else:
                    total[g, 8 : 8 + GROUP, :] += product[g * GROUP : (g + 1) * GROUP]

        def mix(j, low, c, target):
            cols = slice(low, low + WIDTHS[j])
            tap = [taps[core, k : k + 1, begin(half, j)] for k in range(4)]
            for u in range(2):
                group = u * 2 + c
                for r in range(0, GROUP, 32):
                    mixed = total[group, 8 + r : 40 + r, cols]
                    mixed = mixed + tap[0] * mixed
                    for k in range(1, 4):
                        mixed = mixed + tap[k] * total[group, 8 + r - k : 40 + r - k, cols]
                    active = mixed / (1.0 + jnp.exp(-mixed))
                    target[u, r : r + 32, :] = jnp.where(core == 0, active, mixed)

        for n, j in enumerate(parts):
            mix(j, 128 * n, mate, outgoing[j])
            post(outgoing[j], incoming[j], swap_sem.at[j], sibling, lambda j=j: outgoing[j], guard)
        for n, j in enumerate(parts):
            mix(j, 128 * n, core, kept[j])

    def compute_rest():
        pl.when(half == 0)(lambda: compute((1, 2), half))
        pl.when(half == 1)(lambda: compute((1,), other_half))

    def store(j):
        return pltpu.make_async_copy(result[j].at[upper], out.at[:, begin(half, j)], local_sem.at[4 * PARTS + 1 + j])

    def finish(j):
        def body():
            landed(incoming[j], swap_sem.at[j])
            result[j][...] = (kept[j][...] * incoming[j][...]).astype(jnp.bfloat16)
            post(result[j].at[1 - upper], out.at[:, begin(half, j)], back_sem.at[j], at_z(z_rows, core), lambda: result[j].at[0], guard_of(j, half))
            store(j).start()

        present(j, half, body)

    row_copy.wait()
    line_start()
    staged(0)
    send_own(0)
    spread_own(0)
    for j in range(1, PARTS):
        staged(j)
        if j < WINDOW:
            send_own(j)
        spread_own(j)
    side(0, z_hi)
    line_step(1)
    from_rows(0)
    line_step(2)
    from_same(0)
    line_step(3)
    side(0, z_rows)
    side(0, z_same)
    line_step(4)
    side(1, z_hi)
    from_across(0)
    line_step(5)
    from_rows(1)
    from_same(1)
    line_step(6)
    side(2, z_hi)
    ring_relay(upper)
    from_rows(2)
    from_same(2)
    line_step(7)
    side(0, z_across)
    side(1, z_rows)
    side(1, z_same)
    from_across(1)
    ring_relay(1 - upper)
    from_across(2)
    side(2, z_rows)
    side(2, z_same)
    ring_end(upper)
    side(1, z_across)
    side(2, z_across)
    ring_end(1 - upper)
    tokens_end()
    compute((0,), None)
    finish(0)
    compute_rest()
    finish(1)
    finish(2)
    settle()
    line_settle()
    for j in range(PARTS):
        present(j, half, lambda j=j: store(j).wait())
    for j in range(PARTS):
        present(j, 1 - half, lambda j=j: landed(out.at[:, begin(1 - half, j)], back_sem.at[j]))


def on_device(tokens, gate_weight, up_weight, canon_taps):
    anywhere = pl.BlockSpec(memory_space=pl.ANY)
    slots = 32
    scratch = [pltpu.VMEM((slots, 128, w), jnp.bfloat16) for w in WIDTHS]
    for _ in range(3):
        scratch += [pltpu.VMEM((128, w), jnp.bfloat16) for w in WIDTHS]
    for _ in range(3):
        scratch += [pltpu.VMEM((2, GROUP, w), jnp.float32) for w in WIDTHS]
    scratch += [pltpu.VMEM((2, GROUP, w), jnp.bfloat16) for w in WIDTHS]
    scratch += [
        pltpu.VMEM((4 * GROUP, DEPTH), jnp.bfloat16),
        pltpu.VMEM((4, GROUP + 8, 256), jnp.float32),
        pltpu.VMEM((4, GROUP + 8, 128), jnp.float32),
        pltpu.SemaphoreType.DMA((5 * PARTS + 1,)),
        pltpu.SemaphoreType.DMA((SENDS,)),
        pltpu.SemaphoreType.DMA((slots, PARTS)),
        pltpu.SemaphoreType.DMA((8,)),
        pltpu.SemaphoreType.DMA((14,)),
        pltpu.SemaphoreType.DMA((8, 2)),
        pltpu.SemaphoreType.DMA((8, 2)),
        pltpu.SemaphoreType.DMA((2, 2)),
        pltpu.SemaphoreType.DMA((2, 4)),
        pltpu.SemaphoreType.DMA((PARTS,)),
        pltpu.SemaphoreType.DMA((PARTS,)),
    ]
    return pl.pallas_call(
        kernel,
        out_shape=jax.ShapeDtypeStruct((GROUP, gate_weight.shape[1]), jnp.bfloat16),
        in_specs=[anywhere, anywhere, anywhere, pl.BlockSpec(memory_space=pltpu.VMEM)],
        out_specs=anywhere,
        scratch_shapes=scratch,
        compiler_params=pltpu.CompilerParams(collective_id=0, has_side_effects=True, vmem_limit_bytes=56 * 1024 * 1024),
        cost_estimate=pl.CostEstimate(flops=2 * 1024 * 4096 * 512, bytes_accessed=1 << 20, transcendentals=512 * 896),
    )(tokens, gate_weight, up_weight, canon_taps)


def solution(mesh):
    in_specs = (P(("fsdp", "tp"), None), P("fsdp", "tp"), P("fsdp", "tp"), P(None, None, "tp"))
    return jax.shard_map(on_device, mesh=mesh, in_specs=in_specs, out_specs=P("fsdp", "tp"), check_vma=False)
```

```python
import jax
import jax.numpy as jnp
from jax import lax
from jax.experimental import pallas as pl
from jax.experimental.pallas import tpu as pltpu
from jax.sharding import PartitionSpec as P

MESH = pl.DeviceIdType.MESH
WIDTHS = (256, 128, 128)
OFFSETS = (0, 256, 384)
PARTS = len(WIDTHS)
SENDS = 160
DEPTH = 4096
GROUP = 256
STEP = 2048
WINDOW = 3


def kernel(tokens, gate_w, up_w, taps_in, out, *scratch):
    weights = scratch[:PARTS]
    other = scratch[PARTS : 2 * PARTS]
    away = scratch[2 * PARTS : 3 * PARTS]
    other_away = scratch[3 * PARTS : 4 * PARTS]
    outgoing = scratch[4 * PARTS : 5 * PARTS]
    incoming = scratch[5 * PARTS : 6 * PARTS]
    kept = scratch[6 * PARTS : 7 * PARTS]
    result = scratch[7 * PARTS : 8 * PARTS]
    taps, rows, total_wide, total_thin, local_sem, send_sem, weight_sem, run_sem, run_send_sem, ring_sem, ring_send_sem, far_sem, pair_sem, swap_sem, back_sem = scratch[
        8 * PARTS :
    ]

    f, t = lax.axis_index("fsdp"), lax.axis_index("tp")
    core = f % 2
    mate = 1 - core
    x = (f // 2) % 4
    z_hi = f // 8
    z_lo = t % 4
    y = t // 4
    half = (z_hi // 2 + z_lo) % 2
    other_half = 1 - half
    upper = 1 - z_hi % 2
    position = upper * 4 + z_lo
    z_same = (z_hi + 2 * upper - 1 + 4) % 4
    z_rows = (z_hi - 2 * upper + 1 + 4) % 4
    z_across = (z_hi + 2) % 4
    z = z_hi * 4 + z_lo

    def slot(zz, dx, c):
        return (zz * 4 + (x + dx + 4) % 4) * 2 + c

    def at_z(zz, c):
        return (slot(zz, 0, c), t)

    def along_x(d, c):
        return (slot(z_hi, d, c), t)

    def along_y(d):
        return (f, ((y + d + 4) % 4) * 4 + z_lo)

    def along_line(d):
        there = (z + d + 16) % 16
        return (slot(there // 4, 0, core), y * 4 + there % 4)

    sibling = at_z(z_hi, mate)

    def present(j, of_half, body):
        if j < 2:
            body()
        else:
            pl.when(of_half == 0)(body)

    def begin(of_half, j):
        return pl.ds(pl.multiple_of(of_half * 512 + OFFSETS[j], 128), WIDTHS[j])

    def row_at(q):
        return pl.ds(pl.multiple_of((q // 4) * 512 + core * GROUP + y * 64 + (q % 4) * 16, 16), 16)

    row_copy = pltpu.make_async_copy(tokens, rows.at[row_at(position)], local_sem.at[4 * PARTS])
    row_copy.start()
    tap_copy = pltpu.make_async_copy(taps_in, taps, local_sem.at[5 * PARTS + 1])
    tap_copy.start()

    def stage(j, mine, theirs):
        def near():
            pltpu.make_async_copy(mine.at[:, begin(half, j)], weights[j].at[f], local_sem.at[4 * j]).start()
            pltpu.make_async_copy(theirs.at[:, begin(half, j)], other[j], local_sem.at[4 * j + 1]).start()

        def far():
            pltpu.make_async_copy(mine.at[:, begin(1 - half, j)], away[j], local_sem.at[4 * j + 2]).start()
            pltpu.make_async_copy(theirs.at[:, begin(1 - half, j)], other_away[j], local_sem.at[4 * j + 3]).start()

        present(j, half, near)
        present(j, 1 - half, far)

    @pl.when(core == 0)
    def _():
        for j in range(PARTS):
            stage(j, gate_w, up_w)

    @pl.when(core == 1)
    def _():
        for j in range(PARTS):
            stage(j, up_w, gate_w)

    def staged(j):
        def near():
            pltpu.make_async_copy(gate_w.at[:, begin(half, j)], weights[j].at[f], local_sem.at[4 * j]).wait()
            pltpu.make_async_copy(gate_w.at[:, begin(half, j)], other[j], local_sem.at[4 * j + 1]).wait()

        def far():
            pltpu.make_async_copy(gate_w.at[:, begin(1 - half, j)], away[j], local_sem.at[4 * j + 2]).wait()
            pltpu.make_async_copy(gate_w.at[:, begin(1 - half, j)], other_away[j], local_sem.at[4 * j + 3]).wait()

        present(j, half, near)
        present(j, 1 - half, far)

    barrier = pltpu.get_barrier_semaphore()
    partners = [sibling]
    for c in (core, mate):
        partners += [at_z(z_same, c), at_z(z_rows, c), along_x(1, c), along_x(-1, c)]
    partners += [along_line(1), along_line(-1), along_y(1), along_y(-1)]
    for device in partners:
        pl.semaphore_signal(barrier, inc=1, device_id=device, device_id_type=MESH)
    pl.semaphore_wait(barrier, len(partners))

    counter = [0]
    pending = []

    def remote(src, dst, leave, arrive, device):
        return pltpu.make_async_remote_copy(
            src_ref=src, dst_ref=dst, send_sem=leave, recv_sem=arrive, device_id=device, device_id_type=MESH
        )

    def post(src, dst, arrive, device, like, guard=None):
        copy = remote(src, dst, send_sem.at[counter[0]], arrive, device)
        pending.append((guard, counter[0], like))
        counter[0] += 1
        copy.start()

    def landed(ref, arrive):
        remote(ref, ref, send_sem.at[0], arrive, sibling).wait_recv()

    def settle():
        for guard, index, like in pending:
            copy = remote(like(), like(), send_sem.at[index], send_sem.at[index], sibling)
            if guard is None:
                copy.wait_send()
            else:
                pl.when(guard == 0)(copy.wait_send)
        pending.clear()

    def guard_of(j, of_half):
        return None if j < 2 else of_half

    def send_own(j):
        def near():
            guard = guard_of(j, half)
            mine, arrive = weights[j].at[f], weight_sem.at[f, j]
            post(mine, mine, arrive, at_z(z_same, core), lambda: weights[j].at[0], guard)
            post(other[j], mine, arrive, at_z(z_same, mate), lambda: weights[j].at[0], guard)

        def far():
            guard = guard_of(j, other_half)
            post(away[j], weights[j].at[f], weight_sem.at[f, j], at_z(z_rows, core), lambda: weights[j].at[0], guard)
            post(other_away[j], weights[j].at[f], weight_sem.at[f, j], at_z(z_rows, mate), lambda: weights[j].at[0], guard)

        present(j, half, near)
        present(j, 1 - half, far)

    def spread_own(j):
        def body():
            guard = guard_of(j, half)
            mine, arrive = weights[j].at[f], weight_sem.at[f, j]
            for d in (1, -1):
                post(mine, mine, arrive, along_x(d, core), lambda: weights[j].at[0], guard)
                post(other[j], mine, arrive, along_x(d, mate), lambda: weights[j].at[0], guard)
            post(other[j], mine, arrive, sibling, lambda: weights[j].at[0], guard)

        present(j, half, body)

    def pair(j, zz, dx):
        at = slot(zz, dx, 0)
        return weights[j].at[pl.ds(at, 2)], weight_sem.at[at, j]

    def both(j, zz, dx):
        for c in (core, mate):
            landed(weights[j].at[slot(zz, dx, c)], weight_sem.at[slot(zz, dx, c), j])

    def spread(j, zz):
        ref, arrive = pair(j, zz, 0)
        for d in (1, -1):
            post(ref, ref, arrive, along_x(d, core), lambda: weights[j].at[pl.ds(0, 2)], guard_of(j, half))

    def from_rows(j):
        def body():
            both(j, z_rows, 0)
            ref, arrive = pair(j, z_rows, 0)
            post(ref, ref, arrive, at_z(z_same, core), lambda: weights[j].at[pl.ds(0, 2)], guard_of(j, half))
            spread(j, z_rows)

        present(j, half, body)

    def from_same(j):
        def body():
            both(j, z_same, 0)
            spread(j, z_same)

        present(j, half, body)

    def from_across(j):
        def body():
            landed(*pair(j, z_across, 0))
            spread(j, z_across)

        present(j, half, body)

    def side(j, zz):
        def body():
            for d, c in ((1, core), (-1, mate)):
                if zz is z_hi:
                    both(j, z_hi, -d)
                else:
                    landed(*pair(j, zz, -d))
                at = slot(zz, -d, c)
                ref = weights[j].at[at]
                post(ref, ref, weight_sem.at[at, j], along_x(d, core), lambda: weights[j].at[0], guard_of(j, half))

        present(j, half, body)

    def gathered(j):
        landed(weights[j].at[slot(z_hi, 0, mate)], weight_sem.at[slot(z_hi, 0, mate), j])
        for zz in (z_hi, z_rows, z_same, z_across):
            both(j, zz, 2)

    ring = (1, -1)
    line_sends = []

    def line_copy(q, d, index):
        ref = rows.at[row_at(q)]
        return remote(ref, ref, run_send_sem.at[index], run_sem.at[q], along_line(d))

    def ring_copy(q, way):
        ref = rows.at[row_at(q)]
        return remote(ref, ref, ring_send_sem.at[q, way], ring_sem.at[q, way], along_y(ring[way]))

    def line_send(condition, q, d, index):
        pl.when(condition)(lambda: line_copy(q, d, index).start())
        line_sends.append((condition, q, d, index))

    def take(condition, q):
        @pl.when(condition)
        def _():
            landed(rows.at[row_at(q)], run_sem.at[q])

    def give(condition, q):
        @pl.when(condition)
        def _():
            for way in range(2):
                ring_copy(q, way).start()

    def line_start():
        line_send(position < 7, position, 1, 0)
        line_send(position > 0, position, -1, 1)
        for way in range(2):
            ring_copy(position, way).start()

    def line_step(d):
        take(position >= d, position - d)
        if d < 7:
            line_send((position >= d) & (position < 7), position - d, 1, 2 * d)
        take(position + d <= 7, position + d)
        if d < 7:
            line_send((position + d <= 7) & (position > 0), position + d, -1, 2 * d + 1)
        give(position >= d, position - d)
        give(position + d <= 7, position + d)

    def line_settle():
        for condition, q, d, index in line_sends:
            pl.when(condition)(line_copy(q, d, index).wait_send)

        def wait_ring(q, carry):
            for way in range(2):
                ring_copy(q, way).wait_send()
            return carry

        lax.fori_loop(0, 8, wait_ring, 0)

    def block(u, c, dy):
        return rows.at[pl.ds(pl.multiple_of(u * 512 + c * GROUP + ((y + dy + 4) % 4) * 64, 64), 64)]

    def to_mate(u, index, dy):
        post(block(u, core, dy), block(u, core, dy), pair_sem.at[u, index], sibling, lambda: rows.at[pl.ds(0, 64)])

    def far_half(u, dy, way):
        at = u * 512 + core * GROUP + ((y + dy + 4) % 4) * 64 + 32 * way
        return rows.at[pl.ds(pl.multiple_of(at, 32), 32)]

    def ring_relay(u):
        for way, d in enumerate(ring):
            for i in range(4):
                at = u * 512 + core * GROUP + ((y - d + 4) % 4) * 64 + i * 16
                landed(rows.at[pl.ds(pl.multiple_of(at, 16), 16)], ring_sem.at[u * 4 + i, way])
            ref = far_half(u, -d, way)
            post(ref, ref, far_sem.at[u, way], along_y(d), lambda: rows.at[pl.ds(0, 32)])
        to_mate(u, 3, 0)
        for way, d in enumerate(ring):
            to_mate(u, way, -d)

    def ring_end(u):
        for way in range(2):
            landed(far_half(u, 2, way), far_sem.at[u, way])
        to_mate(u, 2, 2)

    def tokens_end():
        for u in range(2):
            for index, dy in enumerate((-1, 1, 2, 0)):
                landed(block(u, mate, dy), pair_sem.at[u, index])

    def compute(parts, guard):
        width = sum(WIDTHS[j] for j in parts)
        total = total_wide if width == 256 else total_thin
        for j in parts:
            gathered(j)
        for g in range(4):
            total[g, 0:8, :] = jnp.zeros((8, width), jnp.float32)
        for i in range(0, DEPTH, STEP):
            pieces = [weights[j][i // 128 : (i + STEP) // 128].reshape(STEP, WIDTHS[j]) for j in parts]
            part = pieces[0] if len(pieces) == 1 else jnp.concatenate(pieces, axis=1)
            product = jnp.dot(rows[:, i : i + STEP], part, preferred_element_type=jnp.float32)
            for g in range(4):
                if i == 0:
                    total[g, 8 : 8 + GROUP, :] = product[g * GROUP : (g + 1) * GROUP]
                else:
                    total[g, 8 : 8 + GROUP, :] += product[g * GROUP : (g + 1) * GROUP]

        def mix(j, low, c, target):
            cols = slice(low, low + WIDTHS[j])
            tap = [taps[core, k : k + 1, begin(half, j)] for k in range(4)]
            for u in range(2):
                group = u * 2 + c
                for r in range(0, GROUP, 32):
                    mixed = total[group, 8 + r : 40 + r, cols]
                    mixed = mixed + tap[0] * mixed
                    for k in range(1, 4):
                        mixed = mixed + tap[k] * total[group, 8 + r - k : 40 + r - k, cols]
                    active = mixed / (1.0 + jnp.exp(-mixed))
                    target[u, r : r + 32, :] = jnp.where(core == 0, active, mixed)

        for n, j in enumerate(parts):
            mix(j, 128 * n, mate, outgoing[j])
            post(outgoing[j], incoming[j], swap_sem.at[j], sibling, lambda j=j: outgoing[j], guard)
        for n, j in enumerate(parts):
            mix(j, 128 * n, core, kept[j])

    def compute_rest():
        pl.when(half == 0)(lambda: compute((1, 2), half))
        pl.when(half == 1)(lambda: compute((1,), other_half))

    def store(j):
        return pltpu.make_async_copy(result[j].at[upper], out.at[:, begin(half, j)], local_sem.at[4 * PARTS + 1 + j])

    def finish(j):
        def body():
            landed(incoming[j], swap_sem.at[j])
            result[j][...] = (kept[j][...] * incoming[j][...]).astype(jnp.bfloat16)
            post(result[j].at[1 - upper], out.at[:, begin(half, j)], back_sem.at[j], at_z(z_rows, core), lambda: result[j].at[0], guard_of(j, half))
            store(j).start()

        present(j, half, body)

    row_copy.wait()
    line_start()
    staged(0)
    send_own(0)
    spread_own(0)
    for j in range(1, PARTS):
        staged(j)
        if j < WINDOW:
            send_own(j)
        spread_own(j)
    side(0, z_hi)
    line_step(1)
    from_rows(0)
    line_step(2)
    from_same(0)
    line_step(3)
    side(0, z_rows)
    line_step(4)
    side(0, z_same)
    from_across(0)
    line_step(5)
    from_rows(1)
    from_same(1)
    line_step(6)
    side(1, z_hi)
    ring_relay(upper)
    from_rows(2)
    line_step(7)
    from_same(2)
    side(2, z_hi)
    ring_relay(1 - upper)
    side(0, z_across)
    side(1, z_rows)
    from_across(1)
    from_across(2)
    side(1, z_same)
    side(2, z_rows)
    side(2, z_same)
    ring_end(upper)
    side(1, z_across)
    ring_end(1 - upper)
    side(2, z_across)
    tokens_end()
    tap_copy.wait()
    compute((0,), None)
    finish(0)
    compute_rest()
    finish(1)
    finish(2)
    settle()
    line_settle()
    for j in range(PARTS):
        present(j, half, lambda j=j: store(j).wait())
    for j in range(PARTS):
        present(j, 1 - half, lambda j=j: landed(out.at[:, begin(1 - half, j)], back_sem.at[j]))


def on_device(tokens, gate_weight, up_weight, canon_taps):
    anywhere = pl.BlockSpec(memory_space=pl.ANY)
    slots = 32
    scratch = [pltpu.VMEM((slots, 128, w), jnp.bfloat16) for w in WIDTHS]
    for _ in range(3):
        scratch += [pltpu.VMEM((128, w), jnp.bfloat16) for w in WIDTHS]
    for _ in range(3):
        scratch += [pltpu.VMEM((2, GROUP, w), jnp.float32) for w in WIDTHS]
    scratch += [pltpu.VMEM((2, GROUP, w), jnp.bfloat16) for w in WIDTHS]
    scratch += [
        pltpu.VMEM(canon_taps.shape, jnp.float32),
        pltpu.VMEM((4 * GROUP, DEPTH), jnp.bfloat16),
        pltpu.VMEM((4, GROUP + 8, 256), jnp.float32),
        pltpu.VMEM((4, GROUP + 8, 128), jnp.float32),
        pltpu.SemaphoreType.DMA((5 * PARTS + 2,)),
        pltpu.SemaphoreType.DMA((SENDS,)),
        pltpu.SemaphoreType.DMA((slots, PARTS)),
        pltpu.SemaphoreType.DMA((8,)),
        pltpu.SemaphoreType.DMA((14,)),
        pltpu.SemaphoreType.DMA((8, 2)),
        pltpu.SemaphoreType.DMA((8, 2)),
        pltpu.SemaphoreType.DMA((2, 2)),
        pltpu.SemaphoreType.DMA((2, 4)),
        pltpu.SemaphoreType.DMA((PARTS,)),
        pltpu.SemaphoreType.DMA((PARTS,)),
    ]
    return pl.pallas_call(
        kernel,
        out_shape=jax.ShapeDtypeStruct((GROUP, gate_weight.shape[1]), jnp.bfloat16),
        in_specs=[anywhere] * 4,
        out_specs=anywhere,
        scratch_shapes=scratch,
        compiler_params=pltpu.CompilerParams(collective_id=0, has_side_effects=True, vmem_limit_bytes=56 * 1024 * 1024),
        cost_estimate=pl.CostEstimate(flops=2 * 1024 * 4096 * 512, bytes_accessed=1 << 20, transcendentals=512 * 896),
    )(tokens, gate_weight, up_weight, canon_taps)


def solution(mesh):
    in_specs = (P(("fsdp", "tp"), None), P("fsdp", "tp"), P("fsdp", "tp"), P(None, None, "tp"))
    return jax.shard_map(on_device, mesh=mesh, in_specs=in_specs, out_specs=P("fsdp", "tp"), check_vma=False)
```

```python
import jax
import jax.numpy as jnp
from jax import lax
from jax.experimental import pallas as pl
from jax.experimental.pallas import tpu as pltpu
from jax.sharding import PartitionSpec as P

MESH = pl.DeviceIdType.MESH
WIDTHS = (256, 128, 128)
OFFSETS = (0, 256, 384)
PARTS = len(WIDTHS)
SENDS = 160
DEPTH = 4096
GROUP = 256
STEP = 4096
WINDOW = 3


def kernel(tokens, gate_w, up_w, taps_in, out, *scratch):
    weights = scratch[:PARTS]
    other = scratch[PARTS : 2 * PARTS]
    away = scratch[2 * PARTS : 3 * PARTS]
    other_away = scratch[3 * PARTS : 4 * PARTS]
    outgoing = scratch[4 * PARTS : 5 * PARTS]
    incoming = scratch[5 * PARTS : 6 * PARTS]
    kept = scratch[6 * PARTS : 7 * PARTS]
    result = scratch[7 * PARTS : 8 * PARTS]
    taps, rows, total_wide, total_thin, local_sem, send_sem, weight_sem, run_sem, run_send_sem, ring_sem, ring_send_sem, far_sem, pair_sem, swap_sem, back_sem = scratch[
        8 * PARTS :
    ]

    f, t = lax.axis_index("fsdp"), lax.axis_index("tp")
    core = f % 2
    mate = 1 - core
    x = (f // 2) % 4
    z_hi = f // 8
    z_lo = t % 4
    y = t // 4
    half = (z_hi // 2 + z_lo) % 2
    other_half = 1 - half
    upper = 1 - z_hi % 2
    position = upper * 4 + z_lo
    z_same = (z_hi + 2 * upper - 1 + 4) % 4
    z_rows = (z_hi - 2 * upper + 1 + 4) % 4
    z_across = (z_hi + 2) % 4
    z = z_hi * 4 + z_lo

    def slot(zz, dx, c):
        return (zz * 4 + (x + dx + 4) % 4) * 2 + c

    def at_z(zz, c):
        return (slot(zz, 0, c), t)

    def along_x(d, c):
        return (slot(z_hi, d, c), t)

    def along_y(d):
        return (f, ((y + d + 4) % 4) * 4 + z_lo)

    def along_line(d):
        there = (z + d + 16) % 16
        return (slot(there // 4, 0, core), y * 4 + there % 4)

    sibling = at_z(z_hi, mate)

    def present(j, of_half, body):
        if j < 2:
            body()
        else:
            pl.when(of_half == 0)(body)

    def begin(of_half, j):
        return pl.ds(pl.multiple_of(of_half * 512 + OFFSETS[j], 128), WIDTHS[j])

    def row_at(q):
        return pl.ds(pl.multiple_of((q // 4) * 512 + core * GROUP + y * 64 + (q % 4) * 16, 16), 16)

    row_copy = pltpu.make_async_copy(tokens, rows.at[row_at(position)], local_sem.at[4 * PARTS])
    row_copy.start()
    tap_copy = pltpu.make_async_copy(taps_in, taps, local_sem.at[5 * PARTS + 1])
    tap_copy.start()

    def stage(j, mine, theirs):
        def near():
            pltpu.make_async_copy(mine.at[:, begin(half, j)], weights[j].at[f], local_sem.at[4 * j]).start()
            pltpu.make_async_copy(theirs.at[:, begin(half, j)], other[j], local_sem.at[4 * j + 1]).start()

        def far():
            pltpu.make_async_copy(mine.at[:, begin(1 - half, j)], away[j], local_sem.at[4 * j + 2]).start()
            pltpu.make_async_copy(theirs.at[:, begin(1 - half, j)], other_away[j], local_sem.at[4 * j + 3]).start()

        present(j, half, near)
        present(j, 1 - half, far)

    @pl.when(core == 0)
    def _():
        for j in range(PARTS):
            stage(j, gate_w, up_w)

    @pl.when(core == 1)
    def _():
        for j in range(PARTS):
            stage(j, up_w, gate_w)

    def staged(j):
        def near():
            pltpu.make_async_copy(gate_w.at[:, begin(half, j)], weights[j].at[f], local_sem.at[4 * j]).wait()
            pltpu.make_async_copy(gate_w.at[:, begin(half, j)], other[j], local_sem.at[4 * j + 1]).wait()

        def far():
            pltpu.make_async_copy(gate_w.at[:, begin(1 - half, j)], away[j], local_sem.at[4 * j + 2]).wait()
            pltpu.make_async_copy(gate_w.at[:, begin(1 - half, j)], other_away[j], local_sem.at[4 * j + 3]).wait()

        present(j, half, near)
        present(j, 1 - half, far)

    barrier = pltpu.get_barrier_semaphore()
    partners = [sibling]
    for c in (core, mate):
        partners += [at_z(z_same, c), at_z(z_rows, c), along_x(1, c), along_x(-1, c)]
    partners += [along_line(1), along_line(-1), along_y(1), along_y(-1)]
    for device in partners:
        pl.semaphore_signal(barrier, inc=1, device_id=device, device_id_type=MESH)
    pl.semaphore_wait(barrier, len(partners))

    counter = [0]
    pending = []

    def remote(src, dst, leave, arrive, device):
        return pltpu.make_async_remote_copy(
            src_ref=src, dst_ref=dst, send_sem=leave, recv_sem=arrive, device_id=device, device_id_type=MESH
        )

    def post(src, dst, arrive, device, like, guard=None):
        copy = remote(src, dst, send_sem.at[counter[0]], arrive, device)
        pending.append((guard, counter[0], like))
        counter[0] += 1
        copy.start()

    def landed(ref, arrive):
        remote(ref, ref, send_sem.at[0], arrive, sibling).wait_recv()

    def settle():
        for guard, index, like in pending:
            copy = remote(like(), like(), send_sem.at[index], send_sem.at[index], sibling)
            if guard is None:
                copy.wait_send()
            else:
                pl.when(guard == 0)(copy.wait_send)
        pending.clear()

    def guard_of(j, of_half):
        return None if j < 2 else of_half

    def send_own(j):
        def near():
            guard = guard_of(j, half)
            mine, arrive = weights[j].at[f], weight_sem.at[f, j]
            post(mine, mine, arrive, at_z(z_same, core), lambda: weights[j].at[0], guard)
            post(other[j], mine, arrive, at_z(z_same, mate), lambda: weights[j].at[0], guard)

        def far():
            guard = guard_of(j, other_half)
            post(away[j], weights[j].at[f], weight_sem.at[f, j], at_z(z_rows, core), lambda: weights[j].at[0], guard)
            post(other_away[j], weights[j].at[f], weight_sem.at[f, j], at_z(z_rows, mate), lambda: weights[j].at[0], guard)

        present(j, half, near)
        present(j, 1 - half, far)

    def spread_own(j):
        def body():
            guard = guard_of(j, half)
            mine, arrive = weights[j].at[f], weight_sem.at[f, j]
            for d in (1, -1):
                post(mine, mine, arrive, along_x(d, core), lambda: weights[j].at[0], guard)
                post(other[j], mine, arrive, along_x(d, mate), lambda: weights[j].at[0], guard)
            post(other[j], mine, arrive, sibling, lambda: weights[j].at[0], guard)

        present(j, half, body)

    def pair(j, zz, dx):
        at = slot(zz, dx, 0)
        return weights[j].at[pl.ds(at, 2)], weight_sem.at[at, j]

    def both(j, zz, dx):
        for c in (core, mate):
            landed(weights[j].at[slot(zz, dx, c)], weight_sem.at[slot(zz, dx, c), j])

    def spread(j, zz):
        ref, arrive = pair(j, zz, 0)
        for d in (1, -1):
            post(ref, ref, arrive, along_x(d, core), lambda: weights[j].at[pl.ds(0, 2)], guard_of(j, half))

    def from_rows(j):
        def body():
            both(j, z_rows, 0)
            ref, arrive = pair(j, z_rows, 0)
            post(ref, ref, arrive, at_z(z_same, core), lambda: weights[j].at[pl.ds(0, 2)], guard_of(j, half))
            spread(j, z_rows)

        present(j, half, body)

    def from_same(j):
        def body():
            both(j, z_same, 0)
            spread(j, z_same)

        present(j, half, body)

    def from_across(j):
        def body():
            landed(*pair(j, z_across, 0))
            spread(j, z_across)

        present(j, half, body)

    def side(j, zz):
        def body():
            for d, c in ((1, core), (-1, mate)):
                if zz is z_hi:
                    both(j, z_hi, -d)
                else:
                    landed(*pair(j, zz, -d))
                at = slot(zz, -d, c)
                ref = weights[j].at[at]
                post(ref, ref, weight_sem.at[at, j], along_x(d, core), lambda: weights[j].at[0], guard_of(j, half))

        present(j, half, body)

    def gathered(j):
        landed(weights[j].at[slot(z_hi, 0, mate)], weight_sem.at[slot(z_hi, 0, mate), j])
        for zz in (z_hi, z_rows, z_same, z_across):
            both(j, zz, 2)

    ring = (1, -1)
    line_sends = []

    def line_copy(q, d, index):
        ref = rows.at[row_at(q)]
        return remote(ref, ref, run_send_sem.at[index], run_sem.at[q], along_line(d))

    def ring_copy(q, way):
        ref = rows.at[row_at(q)]
        return remote(ref, ref, ring_send_sem.at[q, way], ring_sem.at[q, way], along_y(ring[way]))

    def line_send(condition, q, d, index):
        pl.when(condition)(lambda: line_copy(q, d, index).start())
        line_sends.append((condition, q, d, index))

    def take(condition, q):
        @pl.when(condition)
        def _():
            landed(rows.at[row_at(q)], run_sem.at[q])

    def give(condition, q):
        @pl.when(condition)
        def _():
            for way in range(2):
                ring_copy(q, way).start()

    def line_start():
        line_send(position < 7, position, 1, 0)
        line_send(position > 0, position, -1, 1)
        for way in range(2):
            ring_copy(position, way).start()

    def line_step(d):
        take(position >= d, position - d)
        if d < 7:
            line_send((position >= d) & (position < 7), position - d, 1, 2 * d)
        take(position + d <= 7, position + d)
        if d < 7:
            line_send((position + d <= 7) & (position > 0), position + d, -1, 2 * d + 1)
        give(position >= d, position - d)
        give(position + d <= 7, position + d)

    def line_settle():
        for condition, q, d, index in line_sends:
            pl.when(condition)(line_copy(q, d, index).wait_send)

        def wait_ring(q, carry):
            for way in range(2):
                ring_copy(q, way).wait_send()
            return carry

        lax.fori_loop(0, 8, wait_ring, 0)

    def block(u, c, dy):
        return rows.at[pl.ds(pl.multiple_of(u * 512 + c * GROUP + ((y + dy + 4) % 4) * 64, 64), 64)]

    def to_mate(u, index, dy):
        post(block(u, core, dy), block(u, core, dy), pair_sem.at[u, index], sibling, lambda: rows.at[pl.ds(0, 64)])

    def far_half(u, dy, way):
        at = u * 512 + core * GROUP + ((y + dy + 4) % 4) * 64 + 32 * way
        return rows.at[pl.ds(pl.multiple_of(at, 32), 32)]

    def ring_relay(u):
        for way, d in enumerate(ring):
            for i in range(4):
                at = u * 512 + core * GROUP + ((y - d + 4) % 4) * 64 + i * 16
                landed(rows.at[pl.ds(pl.multiple_of(at, 16), 16)], ring_sem.at[u * 4 + i, way])
            ref = far_half(u, -d, way)
            post(ref, ref, far_sem.at[u, way], along_y(d), lambda: rows.at[pl.ds(0, 32)])
        to_mate(u, 3, 0)
        for way, d in enumerate(ring):
            to_mate(u, way, -d)

    def ring_end(u):
        for way in range(2):
            landed(far_half(u, 2, way), far_sem.at[u, way])
        to_mate(u, 2, 2)

    def tokens_end():
        for u in range(2):
            for index, dy in enumerate((-1, 1, 2, 0)):
                landed(block(u, mate, dy), pair_sem.at[u, index])

    def compute(parts, guard):
        width = sum(WIDTHS[j] for j in parts)
        total = total_wide if width == 256 else total_thin
        for j in parts:
            gathered(j)
        for g in range(4):
            total[g, 0:8, :] = jnp.zeros((8, width), jnp.float32)
        for i in range(0, DEPTH, STEP):
            pieces = [weights[j][i // 128 : (i + STEP) // 128].reshape(STEP, WIDTHS[j]) for j in parts]
            part = pieces[0] if len(pieces) == 1 else jnp.concatenate(pieces, axis=1)
            product = jnp.dot(rows[:, i : i + STEP], part, preferred_element_type=jnp.float32)
            for g in range(4):
                if i == 0:
                    total[g, 8 : 8 + GROUP, :] = product[g * GROUP : (g + 1) * GROUP]
                else:
                    total[g, 8 : 8 + GROUP, :] += product[g * GROUP : (g + 1) * GROUP]

        def mix(j, low, c, target):
            cols = slice(low, low + WIDTHS[j])
            tap = [taps[core, k : k + 1, begin(half, j)] for k in range(4)]
            for u in range(2):
                group = u * 2 + c
                for r in range(0, GROUP, 32):
                    mixed = total[group, 8 + r : 40 + r, cols]
                    mixed = mixed + tap[0] * mixed
                    for k in range(1, 4):
                        mixed = mixed + tap[k] * total[group, 8 + r - k : 40 + r - k, cols]
                    active = mixed / (1.0 + jnp.exp(-mixed))
                    target[u, r : r + 32, :] = jnp.where(core == 0, active, mixed)

        for n, j in enumerate(parts):
            mix(j, 128 * n, mate, outgoing[j])
            post(outgoing[j], incoming[j], swap_sem.at[j], sibling, lambda j=j: outgoing[j], guard)
        for n, j in enumerate(parts):
            mix(j, 128 * n, core, kept[j])

    def compute_rest():
        pl.when(half == 0)(lambda: compute((1, 2), half))
        pl.when(half == 1)(lambda: compute((1,), other_half))

    def store(j):
        return pltpu.make_async_copy(result[j].at[upper], out.at[:, begin(half, j)], local_sem.at[4 * PARTS + 1 + j])

    def finish(j):
        def body():
            landed(incoming[j], swap_sem.at[j])
            result[j][...] = (kept[j][...] * incoming[j][...]).astype(jnp.bfloat16)
            post(result[j].at[1 - upper], out.at[:, begin(half, j)], back_sem.at[j], at_z(z_rows, core), lambda: result[j].at[0], guard_of(j, half))
            store(j).start()

        present(j, half, body)

    row_copy.wait()
    line_start()
    staged(0)
    send_own(0)
    spread_own(0)
    for j in range(1, PARTS):
        staged(j)
        if j < WINDOW:
            send_own(j)
        spread_own(j)
    side(0, z_hi)
    line_step(1)
    from_rows(0)
    line_step(2)
    from_same(0)
    line_step(3)
    side(0, z_rows)
    line_step(4)
    side(0, z_same)
    from_across(0)
    line_step(5)
    from_rows(1)
    from_same(1)
    line_step(6)
    side(1, z_hi)
    ring_relay(upper)
    from_rows(2)
    line_step(7)
    from_same(2)
    side(2, z_hi)
    ring_relay(1 - upper)
    side(0, z_across)
    side(1, z_rows)
    from_across(1)
    from_across(2)
    side(1, z_same)
    side(2, z_rows)
    side(2, z_same)
    ring_end(upper)
    side(1, z_across)
    ring_end(1 - upper)
    side(2, z_across)
    tap_copy.wait()
    tokens_end()
    compute((0,), None)
    finish(0)
    compute_rest()
    finish(1)
    finish(2)
    settle()
    line_settle()
    for j in range(PARTS):
        present(j, half, lambda j=j: store(j).wait())
    for j in range(PARTS):
        present(j, 1 - half, lambda j=j: landed(out.at[:, begin(1 - half, j)], back_sem.at[j]))


def on_device(tokens, gate_weight, up_weight, canon_taps):
    anywhere = pl.BlockSpec(memory_space=pl.ANY)
    slots = 32
    scratch = [pltpu.VMEM((slots, 128, w), jnp.bfloat16) for w in WIDTHS]
    for _ in range(3):
        scratch += [pltpu.VMEM((128, w), jnp.bfloat16) for w in WIDTHS]
    for _ in range(3):
        scratch += [pltpu.VMEM((2, GROUP, w), jnp.float32) for w in WIDTHS]
    scratch += [pltpu.VMEM((2, GROUP, w), jnp.bfloat16) for w in WIDTHS]
    scratch += [
        pltpu.VMEM(canon_taps.shape, jnp.float32),
        pltpu.VMEM((4 * GROUP, DEPTH), jnp.bfloat16),
        pltpu.VMEM((4, GROUP + 8, 256), jnp.float32),
        pltpu.VMEM((4, GROUP + 8, 128), jnp.float32),
        pltpu.SemaphoreType.DMA((5 * PARTS + 2,)),
        pltpu.SemaphoreType.DMA((SENDS,)),
        pltpu.SemaphoreType.DMA((slots, PARTS)),
        pltpu.SemaphoreType.DMA((8,)),
        pltpu.SemaphoreType.DMA((14,)),
        pltpu.SemaphoreType.DMA((8, 2)),
        pltpu.SemaphoreType.DMA((8, 2)),
        pltpu.SemaphoreType.DMA((2, 2)),
        pltpu.SemaphoreType.DMA((2, 4)),
        pltpu.SemaphoreType.DMA((PARTS,)),
        pltpu.SemaphoreType.DMA((PARTS,)),
    ]
    return pl.pallas_call(
        kernel,
        out_shape=jax.ShapeDtypeStruct((GROUP, gate_weight.shape[1]), jnp.bfloat16),
        in_specs=[anywhere] * 4,
        out_specs=anywhere,
        scratch_shapes=scratch,
        compiler_params=pltpu.CompilerParams(collective_id=0, has_side_effects=True, vmem_limit_bytes=56 * 1024 * 1024),
        cost_estimate=pl.CostEstimate(flops=2 * 1024 * 4096 * 512, bytes_accessed=1 << 20, transcendentals=512 * 896),
    )(tokens, gate_weight, up_weight, canon_taps)


def solution(mesh):
    in_specs = (P(("fsdp", "tp"), None), P("fsdp", "tp"), P("fsdp", "tp"), P(None, None, "tp"))
    return jax.shard_map(on_device, mesh=mesh, in_specs=in_specs, out_specs=P("fsdp", "tp"), check_vma=False)
```
